512 devices in a mesh: inp: 64 (over x, y, core), tm: 8 (over z).
Axes of the slice: x: 4, y: 8, z: 8, core: 2. Of those that a mesh axis runs over, the one named last changes fastest.
Arguments:
- volts: bfloat16 [512, 524288], P('inp', 'tm'), may hold values from -6 to 6
Outputs:
- visibilities: float32 [2, 512, 512, 512], P(None, ('inp', 'tm'))
The draws below stay inside these ranges and needn't reach their ends.
All inputs are finite; a program needn't handle non-finite values.
Results may differ from the reference program's by a relative error of at most 0.0047.
Values may be sent and summed in bfloat16 or wider, within the bound.
No kernel may reach another device: no remote copies, remote signals or barrier semaphores. Data moves between devices by JAX's collectives and lax.ppermute only.
A program may use at most 64 MiB of HBM per device.

```python
import math
import jax
import jax.numpy as jnp
from jax import lax

FFT = 1024
TAPS = 4
CHAN = 512
INPUTS = 512
TIME = 512


def block_levels(stream_key, dims, split, low, top_value):
    gain, own = 1.0, jax.random.fold_in(stream_key, 6)
    for dim, parts in split:
        heights = jnp.exp(jax.random.uniform(jax.random.fold_in(own, dim), (parts,), jnp.float32, low / len(split), top_value / len(split)))
        gain = gain * jnp.repeat(heights, dims[dim] // parts).reshape([-1 if axis == dim else 1 for axis in range(len(dims))])
    return gain


def gaussian(key, dims, width, reach, pieces=(), kind=jnp.bfloat16):
    entries = jax.random.normal(key, dims, jnp.float32) * width
    if len(pieces) > 0:
        entries = block_levels(key, dims, pieces, -0.22, 0.18) * entries
    return jnp.clip(entries, min=-reach, max=reach).astype(kind)


def setup_inputs(seed: int = 0) -> dict:
    streams_of = jax.random.split(jax.random.key(seed), 2)
    volts = gaussian(streams_of[0], (INPUTS, TIME * FFT), 1.0, 6.0, ((0, 64), (1, 8)))
    return {"volts": volts}


def filter_taps():
    position = jnp.arange(TAPS * FFT, dtype=jnp.float32)
    shifted = (position + 0.5) / FFT - TAPS / 2
    sinc_part = jnp.sin(jnp.pi * shifted) / (jnp.pi * shifted)
    window = 0.54 - 0.46 * jnp.cos(2.0 * jnp.pi * (position + 0.5) / (TAPS * FFT))
    return (sinc_part * window).reshape(TAPS, FFT)

def twiddle_table(channel_order):
    samples = jnp.arange(FFT, dtype=jnp.int32)
    phase = samples[:, None] * channel_order[None, :].astype(jnp.int32) % FFT
    angle = phase.astype(jnp.float32) * (2.0 * math.pi / FFT)
    scale = 1.0 / math.sqrt(FFT)
    return jnp.stack([jnp.cos(angle) * scale, -jnp.sin(angle) * scale], axis=1).astype(jnp.bfloat16)

def polyphase(extended, coeff):
    spectra_count = extended.shape[1] - (TAPS - 1)
    total = coeff[0][None, None, :] * extended[:, 0:spectra_count, :].astype(jnp.float32)
    for step in range(1, TAPS):
        total = total + coeff[step][None, None, :] * extended[:, step:step + spectra_count, :].astype(jnp.float32)
    return total.astype(jnp.bfloat16)

def reference(volts):
    blocks = volts.reshape(INPUTS, TIME, FFT)
    history = jnp.zeros((INPUTS, TAPS - 1, FFT), jnp.bfloat16)
    extended = jnp.concatenate([history, blocks], axis=1)
    coeff = filter_taps()
    table = twiddle_table(jnp.arange(CHAN, dtype=jnp.int32)).astype(jnp.float32)
    groups = extended.reshape(INPUTS // 8, 8, TIME + TAPS - 1, FFT)

    def one_group(members):
        filtered = polyphase(members, coeff).astype(jnp.float32)
        return jnp.einsum('isn,nqc->qcis', filtered, table, precision=lax.Precision.HIGHEST).astype(jnp.bfloat16)
    spectra = lax.map(one_group, groups)
    spectra = spectra.transpose(2, 1, 0, 3, 4).reshape(CHAN, 2, INPUTS, TIME)

    def one_channel(channel_spec):
        stacked = channel_spec.reshape(2 * INPUTS, TIME).astype(jnp.float32)
        gram = jnp.dot(stacked, stacked.T, precision=lax.Precision.HIGHEST)
        real_part = (gram[:INPUTS, :INPUTS] + gram[INPUTS:, INPUTS:]) / TIME
        imag_part = (gram[INPUTS:, :INPUTS] - gram[:INPUTS, INPUTS:]) / TIME
        return jnp.stack([real_part, imag_part])
    visibilities = lax.map(one_channel, spectra)
    return visibilities.transpose(1, 0, 2, 3)
```

```python
import functools
import math

import jax
import jax.numpy as jnp
from jax import lax
from jax.experimental import pallas as pl
from jax.experimental.pallas import tpu as pltpu
from jax.sharding import PartitionSpec as P

FFT = 1024
TAPS = 4
CHAN = 512
LANES = 128
ROWS = 8
VMEM_LIMIT = 40 * 1024 * 1024
NT = (((1,), (1,)), ((), ()))


def table_kernel(tab_ref, coef_ref, ecos_ref, esin_ref):
    position = (
        lax.broadcasted_iota(jnp.int32, (TAPS, FFT), 0) * FFT
        + lax.broadcasted_iota(jnp.int32, (TAPS, FFT), 1)
    ).astype(jnp.float32)
    shifted = (position + 0.5) / FFT - TAPS / 2
    sinc_part = jnp.sin(jnp.pi * shifted) / (jnp.pi * shifted)
    window = 0.54 - 0.46 * jnp.cos(2.0 * jnp.pi * (position + 0.5) / (TAPS * FFT))
    coef_ref[...] = sinc_part * window

    step = 2.0 * math.pi / FFT
    scale = 1.0 / math.sqrt(FFT)
    groups = CHAN // ROWS
    phase = (
        lax.broadcasted_iota(jnp.int32, (groups, LANES), 0)
        * lax.broadcasted_iota(jnp.int32, (groups, LANES), 1)
        * ROWS
    ) % FFT
    angle = phase.astype(jnp.float32) * step
    ecos_ref[...] = jnp.cos(angle)
    esin_ref[...] = jnp.sin(angle)
    sub = lax.broadcasted_iota(jnp.int32, (ROWS, LANES), 0)
    lane = lax.broadcasted_iota(jnp.int32, (ROWS, LANES), 1)
    angle = (sub * lane).astype(jnp.float32) * step
    gcos = jnp.cos(angle) * scale
    gsin = jnp.sin(angle) * scale
    turns = []
    for j in range(FFT // LANES):
        angle = ((sub * (j * LANES)) % FFT).astype(jnp.float32) * step
        turns.append((jnp.cos(angle), jnp.sin(angle)))

    def pair(p, carry):
        bases = []
        for half in range(2):
            ec = ecos_ref[pl.ds(2 * p + half, 1), :]
            es = esin_ref[pl.ds(2 * p + half, 1), :]
            bases.append((ec * gcos - es * gsin, es * gcos + ec * gsin))
        row = pl.multiple_of(p * 2 * ROWS, 2 * ROWS)
        for j, (tc, ts) in enumerate(turns):
            cols = slice(j * LANES, (j + 1) * LANES)
            real = [bc * tc - bs * ts for bc, bs in bases]
            imag = [-(bs * tc + bc * ts) for bc, bs in bases]
            tab_ref[pl.ds(row, 2 * ROWS), cols] = jnp.concatenate(real, 0).astype(jnp.bfloat16)
            tab_ref[pl.ds(CHAN + row, 2 * ROWS), cols] = jnp.concatenate(imag, 0).astype(jnp.bfloat16)
        return carry

    lax.fori_loop(0, groups // 2, pair, 0)


def make_table():
    return pl.pallas_call(
        table_kernel,
        out_shape=(
            jax.ShapeDtypeStruct((2 * CHAN, FFT), jnp.bfloat16),
            jax.ShapeDtypeStruct((TAPS, FFT), jnp.float32),
        ),
        out_specs=(pl.BlockSpec(memory_space=pltpu.VMEM), pl.BlockSpec(memory_space=pltpu.VMEM)),
        scratch_shapes=[
            pltpu.VMEM((CHAN // ROWS, LANES), jnp.float32),
            pltpu.VMEM((CHAN // ROWS, LANES), jnp.float32),
        ],
        compiler_params=pltpu.CompilerParams(vmem_limit_bytes=VMEM_LIMIT),
        cost_estimate=pl.CostEstimate(flops=4_000_000, bytes_accessed=2_100_000, transcendentals=20_000),
        name="dft_table",
    )()


def spectra_kernel(count, volts_ref, halo_ref, coef_ref, tab_ref, out_ref, part_ref, filt_ref, tile_ref):
    def column(j, carry):
        base = pl.multiple_of(j * LANES, LANES)
        taps = [
            jnp.broadcast_to(coef_ref[pl.ds(k, 1), pl.ds(base, LANES)], (ROWS, LANES)) for k in range(TAPS)
        ]
        past = [
            halo_ref[:, pl.ds(base + k * FFT, LANES)].astype(jnp.float32) for k in range(TAPS - 1)
        ]
        for s in range(count):
            past.append(volts_ref[:, pl.ds(base + s * FFT, LANES)].astype(jnp.float32))
            total = taps[0] * past[0]
            for k in range(1, TAPS):
                total = total + taps[k] * past[k]
            past = past[1:]
            part_ref[pl.ds(s, ROWS, stride=count), :] = total
        filt_ref[:, pl.ds(base, LANES)] = part_ref[...].astype(jnp.bfloat16)
        return carry

    lax.fori_loop(0, FFT // LANES, column, 0)

    chunk = 256
    low = lax.broadcasted_iota(jnp.int32, (chunk, LANES), 1) < LANES // 2
    for h in range(CHAN // chunk):
        parts = [
            lax.dot_general(
                tab_ref[q * CHAN + h * chunk : q * CHAN + (h + 1) * chunk, :],
                filt_ref[...],
                NT,
                preferred_element_type=jnp.float32,
            )
            for q in range(2)
        ]
        for j in range(ROWS // 2):
            re = parts[0][:, j * LANES : (j + 1) * LANES]
            im = parts[1][:, j * LANES : (j + 1) * LANES]
            tile_ref[pl.ds(2 * j, chunk, stride=ROWS), :] = jnp.where(low, re, pltpu.roll(im, LANES // 2, 1))
            tile_ref[pl.ds(2 * j + 1, chunk, stride=ROWS), :] = jnp.where(
                low, pltpu.roll(re, LANES // 2, 1), im
            )
        out_ref[h * chunk * ROWS : (h + 1) * chunk * ROWS, :] = tile_ref[...].astype(jnp.bfloat16)


def make_spectra(volts, halo, coef, table):
    count = volts.shape[1] // FFT
    vmem = pl.BlockSpec(memory_space=pltpu.VMEM)
    return pl.pallas_call(
        functools.partial(spectra_kernel, count),
        out_shape=jax.ShapeDtypeStruct((CHAN * ROWS, LANES), jnp.bfloat16),
        in_specs=[vmem] * 4,
        out_specs=vmem,
        scratch_shapes=[
            pltpu.VMEM((ROWS * count, LANES), jnp.float32),
            pltpu.VMEM((ROWS * count, FFT), jnp.bfloat16),
            pltpu.VMEM((256 * ROWS, LANES), jnp.float32),
        ],
        compiler_params=pltpu.CompilerParams(vmem_limit_bytes=VMEM_LIMIT),
        cost_estimate=pl.CostEstimate(flops=1_100_000_000, bytes_accessed=4_000_000, transcendentals=0),
        name="spectra",
    )(volts, halo, coef, table)


def gram_kernel(scale, block, m_ref, out_ref, turned_ref):
    step = pl.program_id(0)

    @pl.when(step == 0)
    def _():
        rows = m_ref.shape[0]
        low = lax.broadcasted_iota(jnp.int32, (rows, LANES), 1) < LANES // 2
        for k in range(m_ref.shape[1] // LANES):
            cols = slice(k * LANES, (k + 1) * LANES)
            swapped = pltpu.roll(m_ref[:, cols].astype(jnp.float32), LANES // 2, 1)
            turned_ref[:, cols] = jnp.where(low, -swapped, swapped).astype(jnp.bfloat16)

    left = m_ref[pl.ds(pl.multiple_of(step * block, block), block), :]
    out_ref[0, 0] = lax.dot_general(left, m_ref[...], NT, preferred_element_type=jnp.float32) * scale
    out_ref[1, 0] = lax.dot_general(left, turned_ref[...], NT, preferred_element_type=jnp.float32) * scale


def make_gram(m, time_total):
    inputs, depth = m.shape
    block = 128
    return pl.pallas_call(
        functools.partial(gram_kernel, 1.0 / time_total, block),
        grid=(inputs // block,),
        out_shape=jax.ShapeDtypeStruct((2, 1, inputs, inputs), jnp.float32),
        in_specs=[pl.BlockSpec((inputs, depth), lambda i: (0, 0))],
        out_specs=pl.BlockSpec((2, 1, block, inputs), lambda i: (0, 0, i, 0)),
        scratch_shapes=[pltpu.VMEM((inputs, depth), jnp.bfloat16)],
        compiler_params=pltpu.CompilerParams(vmem_limit_bytes=VMEM_LIMIT),
        cost_estimate=pl.CostEstimate(flops=1_100_000_000, bytes_accessed=3_200_000, transcendentals=0),
        name="gram",
    )(m)


def on_device(volts):
    inp_local, samples = volts.shape
    count = samples // FFT
    slabs = lax.axis_size("tm")
    groups = lax.axis_size("inp")
    halo = lax.ppermute(
        volts[:, samples - (TAPS - 1) * FFT :], "tm", [(i, i + 1) for i in range(slabs - 1)]
    )
    table, coef = make_table()
    tiles = make_spectra(volts, halo, coef, table)
    tiles = tiles.reshape(CHAN, inp_local, 2 * count)
    tiles = lax.all_to_all(tiles, ("inp", "tm"), split_axis=0, concat_axis=0, tiled=True)
    m = tiles.reshape(groups, slabs, inp_local, 2 * count).transpose(0, 2, 1, 3)
    m = m.reshape(groups * inp_local, slabs * 2 * count)
    return make_gram(m, slabs * count)


def solution(mesh):
    return jax.shard_map(
        on_device,
        mesh=mesh,
        in_specs=(P("inp", "tm"),),
        out_specs=P(None, ("inp", "tm"), None, None),
        check_vma=False,
    )
```

```python
import functools
import math

import jax
import jax.numpy as jnp
from jax import lax
from jax.experimental import pallas as pl
from jax.experimental.pallas import tpu as pltpu
from jax.sharding import PartitionSpec as P

FFT = 1024
TAPS = 4
CHAN = 512
LANES = 128
ROWS = 8
LOADS = 4
VMEM_LIMIT = 40 * 1024 * 1024
NT = (((1,), (1,)), ((), ()))


def prepare_kernel(count, volts_ref, tab_ref, coef_ref, filt_ref, head_ref, local_ref, part_ref, ecos_ref, esin_ref, sem):
    loads = []
    width = volts_ref.shape[1] // LOADS
    for i in range(LOADS):
        cols = pl.ds(i * width, width)
        loads.append(pltpu.make_async_copy(volts_ref.at[:, cols], local_ref.at[:, cols], sem.at[i]))
        loads[-1].start()

    position = (
        lax.broadcasted_iota(jnp.int32, (TAPS, FFT), 0) * FFT
        + lax.broadcasted_iota(jnp.int32, (TAPS, FFT), 1)
    ).astype(jnp.float32)
    shifted = (position + 0.5) / FFT - TAPS / 2
    sinc_part = jnp.sin(jnp.pi * shifted) / (jnp.pi * shifted)
    window = 0.54 - 0.46 * jnp.cos(2.0 * jnp.pi * (position + 0.5) / (TAPS * FFT))
    coef_ref[...] = sinc_part * window

    step = 2.0 * math.pi / FFT
    scale = 1.0 / math.sqrt(FFT)
    groups = CHAN // ROWS
    phase = (
        lax.broadcasted_iota(jnp.int32, (groups, LANES), 0)
        * lax.broadcasted_iota(jnp.int32, (groups, LANES), 1)
        * ROWS
    ) % FFT
    angle = phase.astype(jnp.float32) * step
    ecos_ref[...] = jnp.cos(angle)
    esin_ref[...] = jnp.sin(angle)
    sub = lax.broadcasted_iota(jnp.int32, (ROWS, LANES), 0)
    lane = lax.broadcasted_iota(jnp.int32, (ROWS, LANES), 1)
    angle = (sub * lane).astype(jnp.float32) * step
    gcos = jnp.cos(angle) * scale
    gsin = jnp.sin(angle) * scale
    half_turns = FFT // LANES // 2
    turns = []
    for j in range(half_turns):
        angle = ((sub * (j * LANES)) % FFT).astype(jnp.float32) * step
        turns.append((jnp.cos(angle), jnp.sin(angle)))
    odd = lax.broadcasted_iota(jnp.int32, (2 * ROWS, LANES), 0) % 2 == 1
    sign = jnp.where(odd, -1.0, 1.0).astype(jnp.bfloat16)

    def pair(p, carry):
        bases = []
        for half in range(2):
            ec = ecos_ref[pl.ds(2 * p + half, 1), :]
            es = esin_ref[pl.ds(2 * p + half, 1), :]
            bases.append((ec * gcos - es * gsin, es * gcos + ec * gsin))
        row = pl.multiple_of(p * 2 * ROWS, 2 * ROWS)
        for j, (tc, ts) in enumerate(turns):
            real = [bc * tc - bs * ts for bc, bs in bases] if j else [bc for bc, bs in bases]
            imag = [-(bs * tc + bc * ts) for bc, bs in bases] if j else [-bs for bc, bs in bases]
            for q, value in enumerate((real, imag)):
                value = jnp.concatenate(value, 0).astype(jnp.bfloat16)
                rows = pl.ds(q * CHAN + row, 2 * ROWS)
                tab_ref[rows, j * LANES : (j + 1) * LANES] = value
                tab_ref[rows, (j + half_turns) * LANES : (j + half_turns + 1) * LANES] = value * sign
        return carry

    lax.fori_loop(0, groups // 2, pair, 0)

    for load in loads:
        load.wait()

    pitch = count + ROWS

    def column(j, carry):
        base = pl.multiple_of(j * LANES, LANES)
        cols = pl.ds(base, LANES)
        taps = [jnp.broadcast_to(coef_ref[pl.ds(k, 1), cols], (ROWS, LANES)) for k in range(TAPS)]
        past = []
        for s in range(count):
            past.append(local_ref[:, pl.ds(base + s * FFT, LANES)].astype(jnp.float32))
            total = taps[TAPS - len(past)] * past[0]
            for k in range(1, len(past)):
                total = total + taps[TAPS - len(past) + k] * past[k]
            if s < TAPS - 1:
                head_ref[pl.ds(s * ROWS, ROWS), cols] = total
            else:
                past = past[1:]
            part_ref[pl.ds(s, ROWS, stride=pitch), :] = total
        for a in range(ROWS):
            filt_ref[a * count : (a + 1) * count, cols] = part_ref[a * pitch : a * pitch + count, :].astype(
                jnp.bfloat16
            )
        return carry

    lax.fori_loop(0, FFT // LANES, column, 0)


def prepare(volts):
    inp_local, samples = volts.shape
    count = samples // FFT
    vmem = pl.BlockSpec(memory_space=pltpu.VMEM)
    return pl.pallas_call(
        functools.partial(prepare_kernel, count),
        out_shape=(
            jax.ShapeDtypeStruct((2 * CHAN, FFT), jnp.bfloat16),
            jax.ShapeDtypeStruct((TAPS, FFT), jnp.float32),
            jax.ShapeDtypeStruct((ROWS * count, FFT), jnp.bfloat16),
            jax.ShapeDtypeStruct(((TAPS - 1) * ROWS, FFT), jnp.float32),
        ),
        in_specs=[pl.BlockSpec(memory_space=pltpu.HBM)],
        out_specs=(vmem,) * 4,
        scratch_shapes=[
            pltpu.VMEM((ROWS, samples), jnp.bfloat16),
            pltpu.VMEM((ROWS * (count + ROWS), LANES), jnp.float32),
            pltpu.VMEM((CHAN // ROWS, LANES), jnp.float32),
            pltpu.VMEM((CHAN // ROWS, LANES), jnp.float32),
            pltpu.SemaphoreType.DMA((LOADS,)),
        ],
        compiler_params=pltpu.CompilerParams(vmem_limit_bytes=VMEM_LIMIT),
        cost_estimate=pl.CostEstimate(flops=8_000_000, bytes_accessed=1_100_000, transcendentals=20_000),
        name="prepare",
    )(pltpu.with_memory_space_constraint(volts, pltpu.HBM))


def spectra_kernel(count, halo_ref, coef_ref, tab_ref, filt_ref, head_ref, out_ref, fixed_ref, row_ref, tile_ref):
    late = TAPS - 1
    first = lax.broadcasted_iota(jnp.int32, (ROWS, LANES), 0) < late
    for j in range(FFT // LANES):
        cols = slice(j * LANES, (j + 1) * LANES)
        before = [
            halo_ref[:, k * FFT + j * LANES : k * FFT + (j + 1) * LANES].astype(jnp.float32) for k in range(late)
        ]
        for s in range(late):
            total = head_ref[s * ROWS : (s + 1) * ROWS, cols]
            for k in range(late - s):
                total = total + coef_ref[k : k + 1, cols] * before[s + k]
            row_ref[pl.ds(s, ROWS, stride=ROWS), :] = total
        for a in range(ROWS):
            own = filt_ref[a * count : a * count + 2 * ROWS, cols].astype(jnp.float32)
            top = jnp.where(first, row_ref[a * ROWS : (a + 1) * ROWS, :], own[:ROWS])
            fixed_ref[a * count : a * count + 2 * ROWS, cols] = jnp.concatenate([top, own[ROWS:]], 0).astype(
                jnp.bfloat16
            )

    chunk = 256
    low = lax.broadcasted_iota(jnp.int32, (chunk, LANES), 1) < LANES // 2
    for h in range(CHAN // chunk):
        parts = [
            lax.dot_general(
                tab_ref[q * CHAN + h * chunk : q * CHAN + (h + 1) * chunk, :],
                fixed_ref[...],
                NT,
                preferred_element_type=jnp.float32,
            )
            for q in range(2)
        ]
        for j in range(ROWS // 2):
            re = parts[0][:, j * LANES : (j + 1) * LANES]
            im = parts[1][:, j * LANES : (j + 1) * LANES]
            tile_ref[pl.ds(2 * j, chunk, stride=ROWS), :] = jnp.where(low, re, pltpu.roll(im, LANES // 2, 1))
            tile_ref[pl.ds(2 * j + 1, chunk, stride=ROWS), :] = jnp.where(
                low, pltpu.roll(re, LANES // 2, 1), im
            )
        out_ref[h * chunk * ROWS : (h + 1) * chunk * ROWS, :] = tile_ref[...].astype(jnp.bfloat16)


def make_spectra(halo, coef, table, filtered, head):
    count = filtered.shape[0] // ROWS
    vmem = pl.BlockSpec(memory_space=pltpu.VMEM)
    return pl.pallas_call(
        functools.partial(spectra_kernel, count),
        out_shape=(
            jax.ShapeDtypeStruct((CHAN * ROWS, LANES), jnp.bfloat16),
            jax.ShapeDtypeStruct(filtered.shape, jnp.bfloat16),
        ),
        in_specs=[vmem] * 5,
        out_specs=(vmem, vmem),
        input_output_aliases={3: 1},
        scratch_shapes=[
            pltpu.VMEM((ROWS * ROWS, LANES), jnp.float32),
            pltpu.VMEM((256 * ROWS, LANES), jnp.float32),
        ],
        compiler_params=pltpu.CompilerParams(vmem_limit_bytes=VMEM_LIMIT),
        cost_estimate=pl.CostEstimate(flops=1_100_000_000, bytes_accessed=4_000_000, transcendentals=0),
        name="spectra",
    )(halo, coef, table, filtered, head)[0]


def gram_kernel(scale, m_ref, out_ref, turned_ref, block_ref, sem):
    inputs, depth = m_ref.shape
    block = inputs // 2
    low = lax.broadcasted_iota(jnp.int32, (inputs, LANES), 1) < LANES // 2
    for k in range(depth // LANES):
        cols = slice(k * LANES, (k + 1) * LANES)
        swapped = pltpu.roll(m_ref[:, cols], LANES // 2, 1)
        turned_ref[:, cols] = jnp.where(low, -swapped, swapped)
    copies = []
    for i in range(2):
        rows = pl.ds(i * block, block)
        left = m_ref[rows, :]
        for part, right_ref in enumerate((m_ref, turned_ref)):
            block_ref[part, 0, rows, :] = (
                lax.dot_general(left, right_ref[...], NT, preferred_element_type=jnp.float32) * scale
            )
            copies.append(
                pltpu.make_async_copy(
                    block_ref.at[part, 0, rows], out_ref.at[part, 0, rows], sem.at[2 * i + part]
                )
            )
            copies[-1].start()
    for copy in copies:
        copy.wait()


def make_gram(m, time_total):
    inputs, depth = m.shape
    shape = (2, 1, inputs, inputs)
    return pl.pallas_call(
        functools.partial(gram_kernel, 1.0 / time_total),
        out_shape=jax.ShapeDtypeStruct(shape, jnp.float32),
        in_specs=[pl.BlockSpec(memory_space=pltpu.VMEM)],
        out_specs=pl.BlockSpec(memory_space=pl.ANY),
        scratch_shapes=[
            pltpu.VMEM((inputs, depth), jnp.bfloat16),
            pltpu.VMEM(shape, jnp.float32),
            pltpu.SemaphoreType.DMA((4,)),
        ],
        compiler_params=pltpu.CompilerParams(vmem_limit_bytes=VMEM_LIMIT),
        cost_estimate=pl.CostEstimate(flops=1_100_000_000, bytes_accessed=3_200_000, transcendentals=0),
        name="gram",
    )(m)


def on_device(volts):
    inp_local, samples = volts.shape
    count = samples // FFT
    slabs = lax.axis_size("tm")
    groups = lax.axis_size("inp")
    halo = lax.ppermute(
        volts[:, samples - (TAPS - 1) * FFT :], "tm", [(i, i + 1) for i in range(slabs - 1)]
    )
    table, coef, filtered, head = prepare(volts)
    tiles = make_spectra(halo, coef, table, filtered, head)
    tiles = tiles.reshape(CHAN, inp_local, 2 * count)
    tiles = lax.all_to_all(tiles, ("inp", "tm"), split_axis=0, concat_axis=0, tiled=True)
    m = tiles.reshape(groups, slabs, inp_local, 2 * count).transpose(0, 2, 1, 3)
    m = m.reshape(groups * inp_local, slabs * 2 * count)
    return make_gram(m, slabs * count)


def solution(mesh):
    return jax.shard_map(
        on_device,
        mesh=mesh,
        in_specs=(P("inp", "tm"),),
        out_specs=P(None, ("inp", "tm"), None, None),
        check_vma=False,
    )
```

```python
import functools
import math

import jax
import jax.numpy as jnp
from jax import lax
from jax.experimental import pallas as pl
from jax.experimental.pallas import tpu as pltpu
from jax.sharding import PartitionSpec as P

FFT = 1024
TAPS = 4
CHAN = 512
LANES = 128
ROWS = 8
LOADS = 4
HALF = FFT // 2
VMEM_LIMIT = 40 * 1024 * 1024
NT = (((1,), (1,)), ((), ()))


def prepare_kernel(count, volts_ref, tab_ref, coef_ref, filt_ref, head_ref, local_ref, part_ref, ecos_ref, esin_ref, sem):
    loads = []
    width = volts_ref.shape[1] // LOADS
    for i in range(LOADS):
        cols = pl.ds(i * width, width)
        loads.append(pltpu.make_async_copy(volts_ref.at[:, cols], local_ref.at[:, cols], sem.at[i]))
        loads[-1].start()

    position = (
        lax.broadcasted_iota(jnp.int32, (TAPS, FFT), 0) * FFT
        + lax.broadcasted_iota(jnp.int32, (TAPS, FFT), 1)
    ).astype(jnp.float32)
    shifted = (position + 0.5) / FFT - TAPS / 2
    sinc_part = jnp.sin(jnp.pi * shifted) / (jnp.pi * shifted)
    window = 0.54 - 0.46 * jnp.cos(2.0 * jnp.pi * (position + 0.5) / (TAPS * FFT))
    coef_ref[...] = sinc_part * window

    step = 2.0 * math.pi / FFT
    scale = 1.0 / math.sqrt(FFT)
    groups = CHAN // 2 // ROWS
    phase = (
        lax.broadcasted_iota(jnp.int32, (groups, LANES), 0)
        * lax.broadcasted_iota(jnp.int32, (groups, LANES), 1)
        * (2 * ROWS)
    ) % FFT
    angle = phase.astype(jnp.float32) * step
    ecos_ref[...] = jnp.cos(angle)
    esin_ref[...] = jnp.sin(angle)
    sub = lax.broadcasted_iota(jnp.int32, (ROWS, LANES), 0)
    lane = lax.broadcasted_iota(jnp.int32, (ROWS, LANES), 1)
    factors = []
    for p in range(2):
        angle = (((2 * sub + p) * lane) % FFT).astype(jnp.float32) * step
        turns = []
        for j in range(1, HALF // LANES):
            turn = (((2 * sub + p) * (j * LANES)) % FFT).astype(jnp.float32) * step
            turns.append((jnp.cos(turn), jnp.sin(turn)))
        factors.append((jnp.cos(angle) * scale, jnp.sin(angle) * scale, turns))

    def pair(r, carry):
        starts = [
            (ecos_ref[pl.ds(2 * r + half, 1), :], esin_ref[pl.ds(2 * r + half, 1), :]) for half in range(2)
        ]
        for p, (gcos, gsin, turns) in enumerate(factors):
            bases = [(ec * gcos - es * gsin, es * gcos + ec * gsin) for ec, es in starts]
            for j in range(HALF // LANES):
                if j:
                    tc, ts = turns[j - 1]
                    real = [bc * tc - bs * ts for bc, bs in bases]
                    imag = [-(bs * tc + bc * ts) for bc, bs in bases]
                else:
                    real = [bc for bc, bs in bases]
                    imag = [-bs for bc, bs in bases]
                for q, value in enumerate((real, imag)):
                    row = pl.multiple_of((2 * p + q) * (CHAN // 2) + r * 2 * ROWS, 2 * ROWS)
                    tab_ref[pl.ds(row, 2 * ROWS), j * LANES : (j + 1) * LANES] = jnp.concatenate(
                        value, 0
                    ).astype(jnp.bfloat16)
        return carry

    lax.fori_loop(0, groups // 2, pair, 0)

    for load in loads:
        load.wait()

    pitch = count + ROWS

    def column(j, carry):
        base = pl.multiple_of(j * LANES, LANES)
        cols = [pl.ds(base + h * HALF, LANES) for h in range(2)]
        taps = [
            [jnp.broadcast_to(coef_ref[pl.ds(k, 1), col], (ROWS, LANES)) for k in range(TAPS)] for col in cols
        ]
        past = [[], []]
        for s in range(count):
            total = []
            for h in range(2):
                past[h].append(local_ref[:, pl.ds(base + s * FFT + h * HALF, LANES)].astype(jnp.float32))
                have = len(past[h])
                value = taps[h][TAPS - have] * past[h][0]
                for k in range(1, have):
                    value = value + taps[h][TAPS - have + k] * past[h][k]
                total.append(value)
                if s < TAPS - 1:
                    head_ref[pl.ds(s * ROWS, ROWS), cols[h]] = value
                else:
                    past[h] = past[h][1:]
            part_ref[pl.ds(s, ROWS, stride=pitch), :] = total[0] + total[1]
            part_ref[pl.ds(ROWS * pitch + s, ROWS, stride=pitch), :] = total[0] - total[1]
        for a in range(2 * ROWS):
            filt_ref[a * count : (a + 1) * count, cols[0]] = part_ref[a * pitch : a * pitch + count, :].astype(
                jnp.bfloat16
            )
        return carry

    lax.fori_loop(0, HALF // LANES, column, 0)


def prepare(volts):
    inp_local, samples = volts.shape
    count = samples // FFT
    vmem = pl.BlockSpec(memory_space=pltpu.VMEM)
    return pl.pallas_call(
        functools.partial(prepare_kernel, count),
        out_shape=(
            jax.ShapeDtypeStruct((2 * CHAN, HALF), jnp.bfloat16),
            jax.ShapeDtypeStruct((TAPS, FFT), jnp.float32),
            jax.ShapeDtypeStruct((2 * ROWS * count, HALF), jnp.bfloat16),
            jax.ShapeDtypeStruct(((TAPS - 1) * ROWS, FFT), jnp.float32),
        ),
        in_specs=[pl.BlockSpec(memory_space=pltpu.HBM)],
        out_specs=(vmem,) * 4,
        scratch_shapes=[
            pltpu.VMEM((ROWS, samples), jnp.bfloat16),
            pltpu.VMEM((2 * ROWS * (count + ROWS), LANES), jnp.float32),
            pltpu.VMEM((CHAN // 2 // ROWS, LANES), jnp.float32),
            pltpu.VMEM((CHAN // 2 // ROWS, LANES), jnp.float32),
            pltpu.SemaphoreType.DMA((LOADS,)),
        ],
        compiler_params=pltpu.CompilerParams(vmem_limit_bytes=VMEM_LIMIT),
        cost_estimate=pl.CostEstimate(flops=8_000_000, bytes_accessed=1_100_000, transcendentals=20_000),
        name="prepare",
    )(pltpu.with_memory_space_constraint(volts, pltpu.HBM))


def spectra_kernel(count, halo_ref, coef_ref, tab_ref, filt_ref, head_ref, out_ref, fixed_ref, row_ref, tile_ref):
    late = TAPS - 1
    first = lax.broadcasted_iota(jnp.int32, (ROWS, LANES), 0) < late
    for j in range(HALF // LANES):
        cols = slice(j * LANES, (j + 1) * LANES)
        totals = []
        for h in range(2):
            base = h * HALF + j * LANES
            before = [
                halo_ref[:, k * FFT + base : k * FFT + base + LANES].astype(jnp.float32) for k in range(late)
            ]
            for s in range(late):
                total = head_ref[s * ROWS : (s + 1) * ROWS, base : base + LANES]
                for k in range(late - s):
                    total = total + coef_ref[k : k + 1, base : base + LANES] * before[s + k]
                totals.append(total)
        for s in range(late):
            row_ref[pl.ds(s, ROWS, stride=ROWS), :] = totals[s] + totals[late + s]
            row_ref[pl.ds(ROWS * ROWS + s, ROWS, stride=ROWS), :] = totals[s] - totals[late + s]
        for a in range(2 * ROWS):
            own = filt_ref[a * count : a * count + 2 * ROWS, cols].astype(jnp.float32)
            top = jnp.where(first, row_ref[a * ROWS : (a + 1) * ROWS, :], own[:ROWS])
            fixed_ref[a * count : a * count + 2 * ROWS, cols] = jnp.concatenate([top, own[ROWS:]], 0).astype(
                jnp.bfloat16
            )

    chunk = CHAN // 2
    low = lax.broadcasted_iota(jnp.int32, (chunk, LANES), 1) < LANES // 2
    for p in range(2):
        parts = [
            lax.dot_general(
                tab_ref[(2 * p + q) * chunk : (2 * p + q + 1) * chunk, :],
                fixed_ref[p * ROWS * count : (p + 1) * ROWS * count, :],
                NT,
                preferred_element_type=jnp.float32,
            )
            for q in range(2)
        ]
        first_row = p * chunk * ROWS
        for j in range(ROWS // 2):
            re = parts[0][:, j * LANES : (j + 1) * LANES]
            im = parts[1][:, j * LANES : (j + 1) * LANES]
            tile_ref[pl.ds(first_row + 2 * j, chunk, stride=ROWS), :] = jnp.where(
                low, re, pltpu.roll(im, LANES // 2, 1)
            )
            tile_ref[pl.ds(first_row + 2 * j + 1, chunk, stride=ROWS), :] = jnp.where(
                low, pltpu.roll(re, LANES // 2, 1), im
            )
    even = tile_ref[: chunk * ROWS, :].reshape(chunk, 1, ROWS, LANES)
    odd = tile_ref[chunk * ROWS :, :].reshape(chunk, 1, ROWS, LANES)
    out_ref[...] = jnp.concatenate([even, odd], 1).reshape(CHAN * ROWS, LANES).astype(jnp.bfloat16)


def make_spectra(halo, coef, table, filtered, head):
    count = filtered.shape[0] // ROWS // 2
    vmem = pl.BlockSpec(memory_space=pltpu.VMEM)
    return pl.pallas_call(
        functools.partial(spectra_kernel, count),
        out_shape=(
            jax.ShapeDtypeStruct((CHAN * ROWS, LANES), jnp.bfloat16),
            jax.ShapeDtypeStruct(filtered.shape, jnp.bfloat16),
        ),
        in_specs=[vmem] * 5,
        out_specs=(vmem, vmem),
        input_output_aliases={3: 1},
        scratch_shapes=[
            pltpu.VMEM((2 * ROWS * ROWS, LANES), jnp.float32),
            pltpu.VMEM((CHAN * ROWS, LANES), jnp.float32),
        ],
        compiler_params=pltpu.CompilerParams(vmem_limit_bytes=VMEM_LIMIT),
        cost_estimate=pl.CostEstimate(flops=540_000_000, bytes_accessed=3_000_000, transcendentals=0),
        name="spectra",
    )(halo, coef, table, filtered, head)[0]


def gram_kernel(scale, m_ref, out_ref, turned_ref, block_ref, sem):
    inputs, depth = m_ref.shape
    block = inputs // 2
    low = lax.broadcasted_iota(jnp.int32, (inputs, LANES), 1) < LANES // 2
    for k in range(depth // LANES):
        cols = slice(k * LANES, (k + 1) * LANES)
        swapped = pltpu.roll(m_ref[:, cols], LANES // 2, 1)
        turned_ref[:, cols] = jnp.where(low, -swapped, swapped)
    copies = []
    for i in range(2):
        rows = pl.ds(i * block, block)
        left = m_ref[rows, :]
        for part, right_ref in enumerate((m_ref, turned_ref)):
            block_ref[part, 0, rows, :] = (
                lax.dot_general(left, right_ref[...], NT, preferred_element_type=jnp.float32) * scale
            )
            copies.append(
                pltpu.make_async_copy(
                    block_ref.at[part, 0, rows], out_ref.at[part, 0, rows], sem.at[2 * i + part]
                )
            )
            copies[-1].start()
    for copy in copies:
        copy.wait()


def make_gram(m, time_total):
    inputs, depth = m.shape
    shape = (2, 1, inputs, inputs)
    return pl.pallas_call(
        functools.partial(gram_kernel, 1.0 / time_total),
        out_shape=jax.ShapeDtypeStruct(shape, jnp.float32),
        in_specs=[pl.BlockSpec(memory_space=pltpu.VMEM)],
        out_specs=pl.BlockSpec(memory_space=pl.ANY),
        scratch_shapes=[
            pltpu.VMEM((inputs, depth), jnp.bfloat16),
            pltpu.VMEM(shape, jnp.float32),
            pltpu.SemaphoreType.DMA((4,)),
        ],
        compiler_params=pltpu.CompilerParams(vmem_limit_bytes=VMEM_LIMIT),
        cost_estimate=pl.CostEstimate(flops=1_100_000_000, bytes_accessed=3_200_000, transcendentals=0),
        name="gram",
    )(m)


def on_device(volts):
    inp_local, samples = volts.shape
    count = samples // FFT
    slabs = lax.axis_size("tm")
    groups = lax.axis_size("inp")
    halo = lax.ppermute(
        volts[:, samples - (TAPS - 1) * FFT :], "tm", [(i, i + 1) for i in range(slabs - 1)]
    )
    table, coef, filtered, head = prepare(volts)
    tiles = make_spectra(halo, coef, table, filtered, head)
    tiles = tiles.reshape(CHAN, inp_local, 2 * count)
    tiles = lax.all_to_all(tiles, ("inp", "tm"), split_axis=0, concat_axis=0, tiled=True)
    m = tiles.reshape(groups, slabs, inp_local, 2 * count).transpose(0, 2, 1, 3)
    m = m.reshape(groups * inp_local, slabs * 2 * count)
    return make_gram(m, slabs * count)


def solution(mesh):
    return jax.shard_map(
        on_device,
        mesh=mesh,
        in_specs=(P("inp", "tm"),),
        out_specs=P(None, ("inp", "tm"), None, None),
        check_vma=False,
    )
```

```python
import functools
import math

import jax
import jax.numpy as jnp
from jax import lax
from jax.experimental import pallas as pl
from jax.experimental.pallas import tpu as pltpu
from jax.sharding import Mesh
from jax.sharding import PartitionSpec as P

FFT = 1024
TAPS = 4
CHAN = 512
LANES = 128
ROWS = 8
LOADS = 4
CORES = 2
HALF = FFT // 2
VMEM_LIMIT = 40 * 1024 * 1024
NT = (((1,), (1,)), ((), ()))


def prepare_kernel(count, volts_ref, tab_ref, coef_ref, filt_ref, head_ref, local_ref, part_ref, ecos_ref, esin_ref, sem):
    loads = []
    width = volts_ref.shape[1] // LOADS
    for i in range(LOADS):
        cols = pl.ds(i * width, width)
        loads.append(pltpu.make_async_copy(volts_ref.at[:, cols], local_ref.at[:, cols], sem.at[i]))
        loads[-1].start()

    position = (
        lax.broadcasted_iota(jnp.int32, (TAPS, FFT), 0) * FFT
        + lax.broadcasted_iota(jnp.int32, (TAPS, FFT), 1)
    ).astype(jnp.float32)
    shifted = (position + 0.5) / FFT - TAPS / 2
    sinc_part = jnp.sin(jnp.pi * shifted) / (jnp.pi * shifted)
    window = 0.54 - 0.46 * jnp.cos(2.0 * jnp.pi * (position + 0.5) / (TAPS * FFT))
    coef_ref[...] = sinc_part * window

    step = 2.0 * math.pi / FFT
    scale = 1.0 / math.sqrt(FFT)
    groups = CHAN // 2 // ROWS
    phase = (
        lax.broadcasted_iota(jnp.int32, (groups, LANES), 0)
        * lax.broadcasted_iota(jnp.int32, (groups, LANES), 1)
        * (2 * ROWS)
    ) % FFT
    angle = phase.astype(jnp.float32) * step
    ecos_ref[...] = jnp.cos(angle)
    esin_ref[...] = jnp.sin(angle)
    sub = lax.broadcasted_iota(jnp.int32, (ROWS, LANES), 0)
    lane = lax.broadcasted_iota(jnp.int32, (ROWS, LANES), 1)
    near = CORES * ROWS // 2 * (sub % CORES) + 2 * (sub // CORES)
    factors = []
    for p in range(2):
        angle = (((near + p) * lane) % FFT).astype(jnp.float32) * step
        turns = []
        for j in range(1, HALF // LANES):
            turn = (((near + p) * (j * LANES)) % FFT).astype(jnp.float32) * step
            turns.append((jnp.cos(turn), jnp.sin(turn)))
        factors.append((jnp.cos(angle) * scale, jnp.sin(angle) * scale, turns))

    def pair(r, carry):
        starts = [
            (ecos_ref[pl.ds(2 * r + half, 1), :], esin_ref[pl.ds(2 * r + half, 1), :]) for half in range(2)
        ]
        for p, (gcos, gsin, turns) in enumerate(factors):
            bases = [(ec * gcos - es * gsin, es * gcos + ec * gsin) for ec, es in starts]
            for j in range(HALF // LANES):
                if j:
                    tc, ts = turns[j - 1]
                    real = [bc * tc - bs * ts for bc, bs in bases]
                    imag = [-(bs * tc + bc * ts) for bc, bs in bases]
                else:
                    real = [bc for bc, bs in bases]
                    imag = [-bs for bc, bs in bases]
                for q, value in enumerate((real, imag)):
                    row = pl.multiple_of((2 * p + q) * (CHAN // 2) + r * 2 * ROWS, 2 * ROWS)
                    tab_ref[pl.ds(row, 2 * ROWS), j * LANES : (j + 1) * LANES] = jnp.concatenate(
                        value, 0
                    ).astype(jnp.bfloat16)
        return carry

    lax.fori_loop(0, groups // 2, pair, 0)

    for load in loads:
        load.wait()

    pitch = count + ROWS

    def column(j, carry):
        base = pl.multiple_of(j * LANES, LANES)
        cols = [pl.ds(base + h * HALF, LANES) for h in range(2)]
        taps = [
            [jnp.broadcast_to(coef_ref[pl.ds(k, 1), col], (ROWS, LANES)) for k in range(TAPS)] for col in cols
        ]
        past = [[], []]
        for s in range(count):
            total = []
            for h in range(2):
                past[h].append(local_ref[:, pl.ds(base + s * FFT + h * HALF, LANES)].astype(jnp.float32))
                have = len(past[h])
                value = taps[h][TAPS - have] * past[h][0]
                for k in range(1, have):
                    value = value + taps[h][TAPS - have + k] * past[h][k]
                total.append(value)
                if s < TAPS - 1:
                    head_ref[pl.ds(s * ROWS, ROWS), cols[h]] = value
                else:
                    past[h] = past[h][1:]
            part_ref[pl.ds(s, ROWS, stride=pitch), :] = total[0] + total[1]
            part_ref[pl.ds(ROWS * pitch + s, ROWS, stride=pitch), :] = total[0] - total[1]
        for a in range(2 * ROWS):
            filt_ref[a * count : (a + 1) * count, cols[0]] = part_ref[a * pitch : a * pitch + count, :].astype(
                jnp.bfloat16
            )
        return carry

    lax.fori_loop(0, HALF // LANES, column, 0)


def prepare(volts):
    inp_local, samples = volts.shape
    count = samples // FFT
    vmem = pl.BlockSpec(memory_space=pltpu.VMEM)
    return pl.pallas_call(
        functools.partial(prepare_kernel, count),
        out_shape=(
            jax.ShapeDtypeStruct((2 * CHAN, HALF), jnp.bfloat16),
            jax.ShapeDtypeStruct((TAPS, FFT), jnp.float32),
            jax.ShapeDtypeStruct((2 * ROWS * count, HALF), jnp.bfloat16),
            jax.ShapeDtypeStruct(((TAPS - 1) * ROWS, FFT), jnp.float32),
        ),
        in_specs=[pl.BlockSpec(memory_space=pltpu.HBM)],
        out_specs=(vmem,) * 4,
        scratch_shapes=[
            pltpu.VMEM((ROWS, samples), jnp.bfloat16),
            pltpu.VMEM((2 * ROWS * (count + ROWS), LANES), jnp.float32),
            pltpu.VMEM((CHAN // 2 // ROWS, LANES), jnp.float32),
            pltpu.VMEM((CHAN // 2 // ROWS, LANES), jnp.float32),
            pltpu.SemaphoreType.DMA((LOADS,)),
        ],
        compiler_params=pltpu.CompilerParams(vmem_limit_bytes=VMEM_LIMIT),
        cost_estimate=pl.CostEstimate(flops=8_000_000, bytes_accessed=1_100_000, transcendentals=20_000),
        name="prepare",
    )(pltpu.with_memory_space_constraint(volts, pltpu.HBM))


def spectra_kernel(count, halo_ref, coef_ref, tab_ref, filt_ref, head_ref, out_ref, fixed_ref, row_ref, tile_ref):
    late = TAPS - 1
    first = lax.broadcasted_iota(jnp.int32, (ROWS, LANES), 0) < late
    for j in range(HALF // LANES):
        cols = slice(j * LANES, (j + 1) * LANES)
        totals = []
        for h in range(2):
            base = h * HALF + j * LANES
            before = [
                halo_ref[:, k * FFT + base : k * FFT + base + LANES].astype(jnp.float32) for k in range(late)
            ]
            for s in range(late):
                total = head_ref[s * ROWS : (s + 1) * ROWS, base : base + LANES]
                for k in range(late - s):
                    total = total + coef_ref[k : k + 1, base : base + LANES] * before[s + k]
                totals.append(total)
        for s in range(late):
            row_ref[pl.ds(s, ROWS, stride=ROWS), :] = totals[s] + totals[late + s]
            row_ref[pl.ds(ROWS * ROWS + s, ROWS, stride=ROWS), :] = totals[s] - totals[late + s]
        for a in range(2 * ROWS):
            own = filt_ref[a * count : a * count + 2 * ROWS, cols].astype(jnp.float32)
            top = jnp.where(first, row_ref[a * ROWS : (a + 1) * ROWS, :], own[:ROWS])
            fixed_ref[a * count : a * count + 2 * ROWS, cols] = jnp.concatenate([top, own[ROWS:]], 0).astype(
                jnp.bfloat16
            )

    chunk = CHAN // 2
    low = lax.broadcasted_iota(jnp.int32, (chunk, LANES), 1) < LANES // 2
    for p in range(2):
        parts = [
            lax.dot_general(
                tab_ref[(2 * p + q) * chunk : (2 * p + q + 1) * chunk, :],
                fixed_ref[p * ROWS * count : (p + 1) * ROWS * count, :],
                NT,
                preferred_element_type=jnp.float32,
            )
            for q in range(2)
        ]
        first_row = p * chunk * ROWS
        for j in range(ROWS // 2):
            re = parts[0][:, j * LANES : (j + 1) * LANES]
            im = parts[1][:, j * LANES : (j + 1) * LANES]
            tile_ref[pl.ds(first_row + 2 * j, chunk, stride=ROWS), :] = jnp.where(
                low, re, pltpu.roll(im, LANES // 2, 1)
            )
            tile_ref[pl.ds(first_row + 2 * j + 1, chunk, stride=ROWS), :] = jnp.where(
                low, pltpu.roll(re, LANES // 2, 1), im
            )
    pairs = (chunk // CORES, 1, CORES * ROWS, LANES)
    even = tile_ref[: chunk * ROWS, :].reshape(pairs)
    odd = tile_ref[chunk * ROWS :, :].reshape(pairs)
    out_ref[...] = jnp.concatenate([even, odd], 1).reshape(CHAN * ROWS, LANES).astype(jnp.bfloat16)


def make_spectra(halo, coef, table, filtered, head):
    count = filtered.shape[0] // ROWS // 2
    vmem = pl.BlockSpec(memory_space=pltpu.VMEM)
    return pl.pallas_call(
        functools.partial(spectra_kernel, count),
        out_shape=(
            jax.ShapeDtypeStruct((CHAN * ROWS, LANES), jnp.bfloat16),
            jax.ShapeDtypeStruct(filtered.shape, jnp.bfloat16),
        ),
        in_specs=[vmem] * 5,
        out_specs=(vmem, vmem),
        input_output_aliases={3: 1},
        scratch_shapes=[
            pltpu.VMEM((2 * ROWS * ROWS, LANES), jnp.float32),
            pltpu.VMEM((CHAN * ROWS, LANES), jnp.float32),
        ],
        compiler_params=pltpu.CompilerParams(vmem_limit_bytes=VMEM_LIMIT),
        cost_estimate=pl.CostEstimate(flops=540_000_000, bytes_accessed=3_000_000, transcendentals=0),
        name="spectra",
    )(halo, coef, table, filtered, head)[0]


def gram_kernel(scale, tiles_ref, out_ref, m_ref, turned_ref, block_ref, sem):
    inputs, depth = m_ref.shape
    block = inputs // 2
    low = lax.broadcasted_iota(jnp.int32, (inputs, LANES), 1) < LANES // 2
    for k in range(depth // LANES):
        cols = slice(k * LANES, (k + 1) * LANES)
        tile = tiles_ref[:, k].reshape(inputs, LANES)
        m_ref[:, cols] = tile
        swapped = pltpu.roll(tile, LANES // 2, 1)
        turned_ref[:, cols] = jnp.where(low, -swapped, swapped)
    copies = []
    for i in range(2):
        rows = pl.ds(i * block, block)
        left = m_ref[rows, :]
        for part, right_ref in enumerate((m_ref, turned_ref)):
            block_ref[part, 0, rows, :] = (
                lax.dot_general(left, right_ref[...], NT, preferred_element_type=jnp.float32) * scale
            )
            copies.append(
                pltpu.make_async_copy(
                    block_ref.at[part, 0, rows], out_ref.at[part, 0, rows], sem.at[2 * i + part]
                )
            )
            copies[-1].start()
    for copy in copies:
        copy.wait()


def make_gram(tiles, time_total):
    chips, slabs, rows, lanes = tiles.shape
    inputs, depth = chips * rows, slabs * lanes
    shape = (2, 1, inputs, inputs)
    return pl.pallas_call(
        functools.partial(gram_kernel, 1.0 / time_total),
        out_shape=jax.ShapeDtypeStruct(shape, jnp.float32),
        in_specs=[pl.BlockSpec(memory_space=pltpu.VMEM)],
        out_specs=pl.BlockSpec(memory_space=pl.ANY),
        scratch_shapes=[
            pltpu.VMEM((inputs, depth), jnp.bfloat16),
            pltpu.VMEM((inputs, depth), jnp.bfloat16),
            pltpu.VMEM(shape, jnp.float32),
            pltpu.SemaphoreType.DMA((4,)),
        ],
        compiler_params=pltpu.CompilerParams(vmem_limit_bytes=VMEM_LIMIT),
        cost_estimate=pl.CostEstimate(flops=1_100_000_000, bytes_accessed=3_200_000, transcendentals=0),
        name="gram",
    )(tiles)


def on_device(volts):
    inp_local, samples = volts.shape
    count = samples // FFT
    slabs = lax.axis_size("tm")
    chips = lax.axis_size("chip")
    halo = lax.ppermute(
        volts[:, samples - (TAPS - 1) * FFT :], "tm", [(i, i + 1) for i in range(slabs - 1)]
    )
    table, coef, filtered, head = prepare(volts)
    tiles = make_spectra(halo, coef, table, filtered, head)
    tiles = tiles.reshape(CHAN, inp_local, 2 * count)
    tiles = lax.all_to_all(tiles, ("chip", "tm", "core"), split_axis=0, concat_axis=0, tiled=True)
    return make_gram(tiles.reshape(chips, slabs, CORES * inp_local, 2 * count), slabs * count)


def solution(mesh):
    groups, slabs = mesh.devices.shape
    split = Mesh(mesh.devices.reshape(groups // CORES, CORES, slabs), ("chip", "core", "tm"))
    return jax.shard_map(
        on_device,
        mesh=split,
        in_specs=(P(("chip", "core"), "tm"),),
        out_specs=P(None, ("chip", "core", "tm"), None, None),
        check_vma=False,
    )
```

```python
import functools
import math

import jax
import jax.numpy as jnp
from jax import lax
from jax.experimental import pallas as pl
from jax.experimental.pallas import tpu as pltpu
from jax.sharding import Mesh
from jax.sharding import PartitionSpec as P

FFT = 1024
TAPS = 4
CHAN = 512
LANES = 128
ROWS = 8
LOADS = 4
CORES = 2
VMEM_LIMIT = 40 * 1024 * 1024
NT = (((1,), (1,)), ((), ()))


def prepare_kernel(count, volts_ref, tab_ref, coef_ref, filt_ref, head_ref, local_ref, part_ref, ecos_ref, esin_ref, sem):
    loads = []
    width = volts_ref.shape[1] // LOADS
    for i in range(LOADS):
        cols = pl.ds(i * width, width)
        loads.append(pltpu.make_async_copy(volts_ref.at[:, cols], local_ref.at[:, cols], sem.at[i]))
        loads[-1].start()

    position = (
        lax.broadcasted_iota(jnp.int32, (TAPS, FFT), 0) * FFT
        + lax.broadcasted_iota(jnp.int32, (TAPS, FFT), 1)
    ).astype(jnp.float32)
    shifted = (position + 0.5) / FFT - TAPS / 2
    sinc_part = jnp.sin(jnp.pi * shifted) / (jnp.pi * shifted)
    window = 0.54 - 0.46 * jnp.cos(2.0 * jnp.pi * (position + 0.5) / (TAPS * FFT))
    coef_ref[...] = sinc_part * window

    step = 2.0 * math.pi / FFT
    scale = 1.0 / math.sqrt(FFT)
    groups = CHAN // (2 * ROWS)
    phase = (
        lax.broadcasted_iota(jnp.int32, (groups, LANES), 0)
        * lax.broadcasted_iota(jnp.int32, (groups, LANES), 1)
        * (2 * ROWS)
    ) % FFT
    angle = phase.astype(jnp.float32) * step
    ecos_ref[...] = jnp.cos(angle)
    esin_ref[...] = jnp.sin(angle)
    sub = lax.broadcasted_iota(jnp.int32, (ROWS, LANES), 0)
    lane = lax.broadcasted_iota(jnp.int32, (ROWS, LANES), 1)
    half_turns = FFT // LANES // 2
    factors = []
    for h in range(2):
        near = ROWS * (sub % CORES) + sub // CORES + h * ROWS // 2
        angle = ((near * lane) % FFT).astype(jnp.float32) * step
        turns = []
        for j in range(half_turns):
            turn = ((near * (j * LANES)) % FFT).astype(jnp.float32) * step
            turns.append((jnp.cos(turn), jnp.sin(turn)))
        factors.append((jnp.cos(angle) * scale, jnp.sin(angle) * scale, turns))
    odd = lax.broadcasted_iota(jnp.int32, (2 * ROWS, LANES), 0) // CORES % 2 == 1
    sign = jnp.where(odd, -1.0, 1.0).astype(jnp.bfloat16)

    def pair(w, carry):
        ec = ecos_ref[pl.ds(w, 1), :]
        es = esin_ref[pl.ds(w, 1), :]
        bases = [(ec * gcos - es * gsin, es * gcos + ec * gsin) for gcos, gsin, _ in factors]
        row = pl.multiple_of(w * 2 * ROWS, 2 * ROWS)
        for j in range(half_turns):
            real, imag = [], []
            for (bc, bs), (_, _, turns) in zip(bases, factors):
                tc, ts = turns[j]
                real.append(bc * tc - bs * ts if j else bc)
                imag.append(-(bs * tc + bc * ts) if j else -bs)
            for q, value in enumerate((real, imag)):
                value = jnp.concatenate(value, 0).astype(jnp.bfloat16)
                rows = pl.ds(q * CHAN + row, 2 * ROWS)
                tab_ref[rows, j * LANES : (j + 1) * LANES] = value
                tab_ref[rows, (j + half_turns) * LANES : (j + half_turns + 1) * LANES] = value * sign
        return carry

    lax.fori_loop(0, groups, pair, 0)

    for load in loads:
        load.wait()

    pitch = count + ROWS

    def column(j, carry):
        base = pl.multiple_of(j * LANES, LANES)
        cols = pl.ds(base, LANES)
        taps = [jnp.broadcast_to(coef_ref[pl.ds(k, 1), cols], (ROWS, LANES)) for k in range(TAPS)]
        past = []
        for s in range(count):
            past.append(local_ref[:, pl.ds(base + s * FFT, LANES)].astype(jnp.float32))
            total = taps[TAPS - len(past)] * past[0]
            for k in range(1, len(past)):
                total = total + taps[TAPS - len(past) + k] * past[k]
            if s < TAPS - 1:
                head_ref[pl.ds(s * ROWS, ROWS), cols] = total
            else:
                past = past[1:]
            part_ref[pl.ds(s, ROWS, stride=pitch), :] = total
        for a in range(ROWS):
            filt_ref[a * count : (a + 1) * count, cols] = part_ref[a * pitch : a * pitch + count, :].astype(
                jnp.bfloat16
            )
        return carry

    lax.fori_loop(0, FFT // LANES, column, 0)


def prepare(volts):
    inp_local, samples = volts.shape
    count = samples // FFT
    vmem = pl.BlockSpec(memory_space=pltpu.VMEM)
    return pl.pallas_call(
        functools.partial(prepare_kernel, count),
        out_shape=(
            jax.ShapeDtypeStruct((2 * CHAN, FFT), jnp.bfloat16),
            jax.ShapeDtypeStruct((TAPS, FFT), jnp.float32),
            jax.ShapeDtypeStruct((ROWS * count, FFT), jnp.bfloat16),
            jax.ShapeDtypeStruct(((TAPS - 1) * ROWS, FFT), jnp.float32),
        ),
        in_specs=[pl.BlockSpec(memory_space=pltpu.HBM)],
        out_specs=(vmem,) * 4,
        scratch_shapes=[
            pltpu.VMEM((ROWS, samples), jnp.bfloat16),
            pltpu.VMEM((ROWS * (count + ROWS), LANES), jnp.float32),
            pltpu.VMEM((CHAN // (2 * ROWS), LANES), jnp.float32),
            pltpu.VMEM((CHAN // (2 * ROWS), LANES), jnp.float32),
            pltpu.SemaphoreType.DMA((LOADS,)),
        ],
        compiler_params=pltpu.CompilerParams(vmem_limit_bytes=VMEM_LIMIT),
        cost_estimate=pl.CostEstimate(flops=8_000_000, bytes_accessed=1_100_000, transcendentals=20_000),
        name="prepare",
    )(pltpu.with_memory_space_constraint(volts, pltpu.HBM))


def spectra_kernel(count, halo_ref, coef_ref, tab_ref, filt_ref, head_ref, out_ref, fixed_ref, row_ref, tile_ref):
    late = TAPS - 1
    first = lax.broadcasted_iota(jnp.int32, (ROWS, LANES), 0) < late
    for j in range(FFT // LANES):
        cols = slice(j * LANES, (j + 1) * LANES)
        before = [
            halo_ref[:, k * FFT + j * LANES : k * FFT + (j + 1) * LANES].astype(jnp.float32) for k in range(late)
        ]
        for s in range(late):
            total = head_ref[s * ROWS : (s + 1) * ROWS, cols]
            for k in range(late - s):
                total = total + coef_ref[k : k + 1, cols] * before[s + k]
            row_ref[pl.ds(s, ROWS, stride=ROWS), :] = total
        for a in range(ROWS):
            own = filt_ref[a * count : a * count + 2 * ROWS, cols].astype(jnp.float32)
            top = jnp.where(first, row_ref[a * ROWS : (a + 1) * ROWS, :], own[:ROWS])
            fixed_ref[a * count : a * count + 2 * ROWS, cols] = jnp.concatenate([top, own[ROWS:]], 0).astype(
                jnp.bfloat16
            )

    chunk = 256
    low = lax.broadcasted_iota(jnp.int32, (chunk, LANES), 1) < LANES // 2
    for h in range(CHAN // chunk):
        parts = [
            lax.dot_general(
                tab_ref[q * CHAN + h * chunk : q * CHAN + (h + 1) * chunk, :],
                fixed_ref[...],
                NT,
                preferred_element_type=jnp.float32,
            )
            for q in range(2)
        ]
        for j in range(ROWS // 2):
            re = parts[0][:, j * LANES : (j + 1) * LANES]
            im = parts[1][:, j * LANES : (j + 1) * LANES]
            tile_ref[pl.ds(2 * j, chunk, stride=ROWS), :] = jnp.where(low, re, pltpu.roll(im, LANES // 2, 1))
            tile_ref[pl.ds(2 * j + 1, chunk, stride=ROWS), :] = jnp.where(
                low, pltpu.roll(re, LANES // 2, 1), im
            )
        out_ref[h * chunk * ROWS : (h + 1) * chunk * ROWS, :] = tile_ref[...].astype(jnp.bfloat16)


def make_spectra(halo, coef, table, filtered, head):
    count = filtered.shape[0] // ROWS
    vmem = pl.BlockSpec(memory_space=pltpu.VMEM)
    return pl.pallas_call(
        functools.partial(spectra_kernel, count),
        out_shape=(
            jax.ShapeDtypeStruct((CHAN * ROWS, LANES), jnp.bfloat16),
            jax.ShapeDtypeStruct(filtered.shape, jnp.bfloat16),
        ),
        in_specs=[vmem] * 5,
        out_specs=(vmem, vmem),
        input_output_aliases={3: 1},
        scratch_shapes=[
            pltpu.VMEM((ROWS * ROWS, LANES), jnp.float32),
            pltpu.VMEM((256 * ROWS, LANES), jnp.float32),
        ],
        compiler_params=pltpu.CompilerParams(vmem_limit_bytes=VMEM_LIMIT),
        cost_estimate=pl.CostEstimate(flops=1_100_000_000, bytes_accessed=4_000_000, transcendentals=0),
        name="spectra",
    )(halo, coef, table, filtered, head)[0]


def gram_kernel(scale, tiles_ref, out_ref, m_ref, turned_ref, block_ref, sem):
    inputs, depth = m_ref.shape
    block = inputs // 2
    low = lax.broadcasted_iota(jnp.int32, (inputs, LANES), 1) < LANES // 2
    for k in range(depth // LANES):
        cols = slice(k * LANES, (k + 1) * LANES)
        tile = tiles_ref[:, k].reshape(inputs, LANES)
        m_ref[:, cols] = tile
        swapped = pltpu.roll(tile, LANES // 2, 1)
        turned_ref[:, cols] = jnp.where(low, -swapped, swapped)
    copies = []
    for i in range(2):
        rows = pl.ds(i * block, block)
        left = m_ref[rows, :]
        for part, right_ref in enumerate((m_ref, turned_ref)):
            block_ref[part, 0, rows, :] = (
                lax.dot_general(left, right_ref[...], NT, preferred_element_type=jnp.float32) * scale
            )
            copies.append(
                pltpu.make_async_copy(
                    block_ref.at[part, 0, rows], out_ref.at[part, 0, rows], sem.at[2 * i + part]
                )
            )
            copies[-1].start()
    for copy in copies:
        copy.wait()


def make_gram(tiles, time_total):
    chips, slabs, rows, lanes = tiles.shape
    inputs, depth = chips * rows, slabs * lanes
    shape = (2, 1, inputs, inputs)
    return pl.pallas_call(
        functools.partial(gram_kernel, 1.0 / time_total),
        out_shape=jax.ShapeDtypeStruct(shape, jnp.float32),
        in_specs=[pl.BlockSpec(memory_space=pltpu.VMEM)],
        out_specs=pl.BlockSpec(memory_space=pl.ANY),
        scratch_shapes=[
            pltpu.VMEM((inputs, depth), jnp.bfloat16),
            pltpu.VMEM((inputs, depth), jnp.bfloat16),
            pltpu.VMEM(shape, jnp.float32),
            pltpu.SemaphoreType.DMA((4,)),
        ],
        compiler_params=pltpu.CompilerParams(vmem_limit_bytes=VMEM_LIMIT),
        cost_estimate=pl.CostEstimate(flops=1_100_000_000, bytes_accessed=3_200_000, transcendentals=0),
        name="gram",
    )(tiles)


def on_device(volts):
    inp_local, samples = volts.shape
    count = samples // FFT
    slabs = lax.axis_size("tm")
    chips = lax.axis_size("chip")
    halo = lax.ppermute(
        volts[:, samples - (TAPS - 1) * FFT :], "tm", [(i, i + 1) for i in range(slabs - 1)]
    )
    table, coef, filtered, head = prepare(volts)
    tiles = make_spectra(halo, coef, table, filtered, head)
    tiles = tiles.reshape(CHAN, inp_local, 2 * count)
    tiles = lax.all_to_all(tiles, ("chip", "tm", "core"), split_axis=0, concat_axis=0, tiled=True)
    return make_gram(tiles.reshape(chips, slabs, CORES * inp_local, 2 * count), slabs * count)


def solution(mesh):
    groups, slabs = mesh.devices.shape
    split = Mesh(mesh.devices.reshape(groups // CORES, CORES, slabs), ("chip", "core", "tm"))
    return jax.shard_map(
        on_device,
        mesh=split,
        in_specs=(P(("chip", "core"), "tm"),),
        out_specs=P(None, ("chip", "core", "tm"), None, None),
        check_vma=False,
    )
```

```python
import functools
import math

import jax
import jax.numpy as jnp
from jax import lax
from jax.experimental import pallas as pl
from jax.experimental.pallas import tpu as pltpu
from jax.sharding import Mesh
from jax.sharding import PartitionSpec as P

FFT = 1024
TAPS = 4
CHAN = 512
LANES = 128
ROWS = 8
LOADS = 4
CORES = 2
HALF = FFT // 2
VMEM_LIMIT = 40 * 1024 * 1024
NT = (((1,), (1,)), ((), ()))


def prepare_kernel(count, volts_ref, tab_ref, coef_ref, filt_ref, head_ref, local_ref, part_ref, ecos_ref, esin_ref, sem):
    loads = []
    width = volts_ref.shape[1] // LOADS
    for i in range(LOADS):
        cols = pl.ds(i * width, width)
        loads.append(pltpu.make_async_copy(volts_ref.at[:, cols], local_ref.at[:, cols], sem.at[i]))
        loads[-1].start()

    position = (
        lax.broadcasted_iota(jnp.int32, (TAPS, FFT), 0) * FFT
        + lax.broadcasted_iota(jnp.int32, (TAPS, FFT), 1)
    ).astype(jnp.float32)
    shifted = (position + 0.5) / FFT - TAPS / 2
    sinc_part = jnp.sin(jnp.pi * shifted) / (jnp.pi * shifted)
    window = 0.54 - 0.46 * jnp.cos(2.0 * jnp.pi * (position + 0.5) / (TAPS * FFT))
    coef_ref[...] = sinc_part * window

    step = 2.0 * math.pi / FFT
    scale = 1.0 / math.sqrt(FFT)
    groups = CHAN // 2 // ROWS
    phase = (
        lax.broadcasted_iota(jnp.int32, (groups, LANES), 0)
        * lax.broadcasted_iota(jnp.int32, (groups, LANES), 1)
        * (2 * ROWS)
    ) % FFT
    angle = phase.astype(jnp.float32) * step
    ecos_ref[...] = jnp.cos(angle)
    esin_ref[...] = jnp.sin(angle)
    sub = lax.broadcasted_iota(jnp.int32, (ROWS, LANES), 0)
    lane = lax.broadcasted_iota(jnp.int32, (ROWS, LANES), 1)
    near = CORES * ROWS // 2 * (sub % CORES) + 2 * (sub // CORES)
    factors = []
    for p in range(2):
        angle = (((near + p) * lane) % FFT).astype(jnp.float32) * step
        turns = []
        for j in range(1, HALF // LANES):
            turn = (((near + p) * (j * LANES)) % FFT).astype(jnp.float32) * step
            turns.append((jnp.cos(turn), jnp.sin(turn)))
        factors.append((jnp.cos(angle) * scale, jnp.sin(angle) * scale, turns))

    def pair(r, carry):
        starts = [
            (ecos_ref[pl.ds(2 * r + half, 1), :], esin_ref[pl.ds(2 * r + half, 1), :]) for half in range(2)
        ]
        for p, (gcos, gsin, turns) in enumerate(factors):
            bases = [(ec * gcos - es * gsin, es * gcos + ec * gsin) for ec, es in starts]
            for j in range(HALF // LANES):
                if j:
                    tc, ts = turns[j - 1]
                    real = [bc * tc - bs * ts for bc, bs in bases]
                    imag = [-(bs * tc + bc * ts) for bc, bs in bases]
                else:
                    real = [bc for bc, bs in bases]
                    imag = [-bs for bc, bs in bases]
                for q, value in enumerate((real, imag)):
                    row = pl.multiple_of((2 * p + q) * (CHAN // 2) + r * 2 * ROWS, 2 * ROWS)
                    tab_ref[pl.ds(row, 2 * ROWS), j * LANES : (j + 1) * LANES] = jnp.concatenate(
                        value, 0
                    ).astype(jnp.bfloat16)
        return carry

    lax.fori_loop(0, groups // 2, pair, 0)

    for load in loads:
        load.wait()

    pitch = count + ROWS

    def column(j, carry):
        base = pl.multiple_of(j * LANES, LANES)
        cols = [pl.ds(base + h * HALF, LANES) for h in range(2)]
        taps = [
            [jnp.broadcast_to(coef_ref[pl.ds(k, 1), col], (ROWS, LANES)) for k in range(TAPS)] for col in cols
        ]
        past = [[], []]
        for s in range(count):
            total = []
            for h in range(2):
                past[h].append(local_ref[:, pl.ds(base + s * FFT + h * HALF, LANES)].astype(jnp.float32))
                have = len(past[h])
                value = taps[h][TAPS - have] * past[h][0]
                for k in range(1, have):
                    value = value + taps[h][TAPS - have + k] * past[h][k]
                total.append(value)
                if s < TAPS - 1:
                    head_ref[pl.ds(s * ROWS, ROWS), cols[h]] = value
                else:
                    past[h] = past[h][1:]
            part_ref[pl.ds(s, ROWS, stride=pitch), :] = total[0] + total[1]
            part_ref[pl.ds(ROWS * pitch + s, ROWS, stride=pitch), :] = total[0] - total[1]
        for a in range(2 * ROWS):
            filt_ref[a * count : (a + 1) * count, cols[0]] = part_ref[a * pitch : a * pitch + count, :].astype(
                jnp.bfloat16
            )
        return carry

    lax.fori_loop(0, HALF // LANES, column, 0)


def prepare(volts):
    inp_local, samples = volts.shape
    count = samples // FFT
    vmem = pl.BlockSpec(memory_space=pltpu.VMEM)
    return pl.pallas_call(
        functools.partial(prepare_kernel, count),
        out_shape=(
            jax.ShapeDtypeStruct((2 * CHAN, HALF), jnp.bfloat16),
            jax.ShapeDtypeStruct((TAPS, FFT), jnp.float32),
            jax.ShapeDtypeStruct((2 * ROWS * count, HALF), jnp.bfloat16),
            jax.ShapeDtypeStruct(((TAPS - 1) * ROWS, FFT), jnp.float32),
        ),
        in_specs=[pl.BlockSpec(memory_space=pltpu.HBM)],
        out_specs=(vmem,) * 4,
        scratch_shapes=[
            pltpu.VMEM((ROWS, samples), jnp.bfloat16),
            pltpu.VMEM(((2 * ROWS + 1) * (count + ROWS), LANES), jnp.float32),
            pltpu.VMEM((CHAN // 2 // ROWS, LANES), jnp.float32),
            pltpu.VMEM((CHAN // 2 // ROWS, LANES), jnp.float32),
            pltpu.SemaphoreType.DMA((LOADS,)),
        ],
        compiler_params=pltpu.CompilerParams(vmem_limit_bytes=VMEM_LIMIT),
        cost_estimate=pl.CostEstimate(flops=8_000_000, bytes_accessed=1_100_000, transcendentals=20_000),
        name="prepare",
    )(pltpu.with_memory_space_constraint(volts, pltpu.HBM))


def spectra_kernel(count, halo_ref, coef_ref, tab_ref, filt_ref, head_ref, out_ref, fixed_ref, row_ref, tile_ref):
    late = TAPS - 1
    first = lax.broadcasted_iota(jnp.int32, (ROWS, LANES), 0) < late
    for j in range(HALF // LANES):
        cols = slice(j * LANES, (j + 1) * LANES)
        totals = []
        for h in range(2):
            base = h * HALF + j * LANES
            before = [
                halo_ref[:, k * FFT + base : k * FFT + base + LANES].astype(jnp.float32) for k in range(late)
            ]
            for s in range(late):
                total = head_ref[s * ROWS : (s + 1) * ROWS, base : base + LANES]
                for k in range(late - s):
                    total = total + coef_ref[k : k + 1, base : base + LANES] * before[s + k]
                totals.append(total)
        for s in range(late):
            row_ref[pl.ds(s, ROWS, stride=ROWS), :] = totals[s] + totals[late + s]
            row_ref[pl.ds(ROWS * ROWS + s, ROWS, stride=ROWS), :] = totals[s] - totals[late + s]
        for a in range(2 * ROWS):
            own = filt_ref[a * count : a * count + 2 * ROWS, cols].astype(jnp.float32)
            top = jnp.where(first, row_ref[a * ROWS : (a + 1) * ROWS, :], own[:ROWS])
            fixed_ref[a * count : a * count + 2 * ROWS, cols] = jnp.concatenate([top, own[ROWS:]], 0).astype(
                jnp.bfloat16
            )

    chunk = CHAN // 2
    low = lax.broadcasted_iota(jnp.int32, (chunk, LANES), 1) < LANES // 2
    for p in range(2):
        parts = [
            lax.dot_general(
                tab_ref[(2 * p + q) * chunk : (2 * p + q + 1) * chunk, :],
                fixed_ref[p * ROWS * count : (p + 1) * ROWS * count, :],
                NT,
                preferred_element_type=jnp.float32,
            )
            for q in range(2)
        ]
        first_row = p * chunk * ROWS
        for j in range(ROWS // 2):
            re = parts[0][:, j * LANES : (j + 1) * LANES]
            im = parts[1][:, j * LANES : (j + 1) * LANES]
            tile_ref[pl.ds(first_row + 2 * j, chunk, stride=ROWS), :] = jnp.where(
                low, re, pltpu.roll(im, LANES // 2, 1)
            )
            tile_ref[pl.ds(first_row + 2 * j + 1, chunk, stride=ROWS), :] = jnp.where(
                low, pltpu.roll(re, LANES // 2, 1), im
            )
    pairs = (chunk // CORES, 1, CORES * ROWS, LANES)
    even = tile_ref[: chunk * ROWS, :].reshape(pairs)
    odd = tile_ref[chunk * ROWS : CHAN * ROWS, :].reshape(pairs)
    out_ref[...] = jnp.concatenate([even, odd], 1).reshape(CHAN * ROWS, LANES).astype(jnp.bfloat16)


def make_spectra(halo, coef, table, filtered, head):
    count = filtered.shape[0] // ROWS // 2
    vmem = pl.BlockSpec(memory_space=pltpu.VMEM)
    return pl.pallas_call(
        functools.partial(spectra_kernel, count),
        out_shape=(
            jax.ShapeDtypeStruct((CHAN * ROWS, LANES), jnp.bfloat16),
            jax.ShapeDtypeStruct(filtered.shape, jnp.bfloat16),
        ),
        in_specs=[vmem] * 5,
        out_specs=(vmem, vmem),
        input_output_aliases={3: 1},
        scratch_shapes=[
            pltpu.VMEM(((2 * ROWS + 1) * ROWS, LANES), jnp.float32),
            pltpu.VMEM(((CHAN + 1) * ROWS, LANES), jnp.float32),
        ],
        compiler_params=pltpu.CompilerParams(vmem_limit_bytes=VMEM_LIMIT),
        cost_estimate=pl.CostEstimate(flops=540_000_000, bytes_accessed=3_000_000, transcendentals=0),
        name="spectra",
    )(halo, coef, table, filtered, head)[0]


def gram_kernel(scale, tiles_ref, out_ref, m_ref, turned_ref, block_ref, sem):
    inputs, depth = m_ref.shape
    block = inputs // 2
    low = lax.broadcasted_iota(jnp.int32, (inputs, LANES), 1) < LANES // 2
    for k in range(depth // LANES):
        cols = slice(k * LANES, (k + 1) * LANES)
        tile = tiles_ref[:, k].reshape(inputs, LANES)
        m_ref[:, cols] = tile
        swapped = pltpu.roll(tile, LANES // 2, 1)
        turned_ref[:, cols] = jnp.where(low, -swapped, swapped)
    copies = []
    for i in range(2):
        rows = pl.ds(i * block, block)
        left = m_ref[rows, :]
        for part, right_ref in enumerate((m_ref, turned_ref)):
            block_ref[part, 0, rows, :] = (
                lax.dot_general(left, right_ref[...], NT, preferred_element_type=jnp.float32) * scale
            )
            copies.append(
                pltpu.make_async_copy(
                    block_ref.at[part, 0, rows], out_ref.at[part, 0, rows], sem.at[2 * i + part]
                )
            )
            copies[-1].start()
    for copy in copies:
        copy.wait()


def make_gram(tiles, time_total):
    chips, slabs, rows, lanes = tiles.shape
    inputs, depth = chips * rows, slabs * lanes
    shape = (2, 1, inputs, inputs)
    return pl.pallas_call(
        functools.partial(gram_kernel, 1.0 / time_total),
        out_shape=jax.ShapeDtypeStruct(shape, jnp.float32),
        in_specs=[pl.BlockSpec(memory_space=pltpu.VMEM)],
        out_specs=pl.BlockSpec(memory_space=pl.ANY),
        scratch_shapes=[
            pltpu.VMEM((inputs, depth), jnp.bfloat16),
            pltpu.VMEM((inputs, depth), jnp.bfloat16),
            pltpu.VMEM(shape, jnp.float32),
            pltpu.SemaphoreType.DMA((4,)),
        ],
        compiler_params=pltpu.CompilerParams(vmem_limit_bytes=VMEM_LIMIT),
        cost_estimate=pl.CostEstimate(flops=1_100_000_000, bytes_accessed=3_200_000, transcendentals=0),
        name="gram",
    )(tiles)


def on_device(volts):
    inp_local, samples = volts.shape
    count = samples // FFT
    slabs = lax.axis_size("tm")
    chips = lax.axis_size("chip")
    halo = lax.ppermute(
        volts[:, samples - (TAPS - 1) * FFT :], "tm", [(i, i + 1) for i in range(slabs - 1)]
    )
    table, coef, filtered, head = prepare(volts)
    tiles = make_spectra(halo, coef, table, filtered, head)
    tiles = tiles.reshape(CHAN, inp_local, 2 * count)
    tiles = lax.all_to_all(tiles, ("chip", "tm", "core"), split_axis=0, concat_axis=0, tiled=True)
    return make_gram(tiles.reshape(chips, slabs, CORES * inp_local, 2 * count), slabs * count)


def solution(mesh):
    groups, slabs = mesh.devices.shape
    split = Mesh(mesh.devices.reshape(groups // CORES, CORES, slabs), ("chip", "core", "tm"))
    return jax.shard_map(
        on_device,
        mesh=split,
        in_specs=(P(("chip", "core"), "tm"),),
        out_specs=P(None, ("chip", "core", "tm"), None, None),
        check_vma=False,
    )
```

```python
import functools
import math

import jax
import jax.numpy as jnp
from jax import lax
from jax.experimental import pallas as pl
from jax.experimental.pallas import tpu as pltpu
from jax.sharding import Mesh
from jax.sharding import PartitionSpec as P

FFT = 1024
TAPS = 4
CHAN = 512
LANES = 128
ROWS = 8
LOADS = 4
CORES = 2
VMEM_LIMIT = 40 * 1024 * 1024
NT = (((1,), (1,)), ((), ()))


def prepare_kernel(count, volts_ref, tab_ref, coef_ref, filt_ref, head_ref, local_ref, part_ref, ecos_ref, esin_ref, sem):
    loads = []
    width = volts_ref.shape[1] // LOADS
    for i in range(LOADS):
        cols = pl.ds(i * width, width)
        loads.append(pltpu.make_async_copy(volts_ref.at[:, cols], local_ref.at[:, cols], sem.at[i]))
        loads[-1].start()

    position = (
        lax.broadcasted_iota(jnp.int32, (TAPS, FFT), 0) * FFT
        + lax.broadcasted_iota(jnp.int32, (TAPS, FFT), 1)
    ).astype(jnp.float32)
    shifted = (position + 0.5) / FFT - TAPS / 2
    sinc_part = jnp.sin(jnp.pi * shifted) / (jnp.pi * shifted)
    window = 0.54 - 0.46 * jnp.cos(2.0 * jnp.pi * (position + 0.5) / (TAPS * FFT))
    coef_ref[...] = sinc_part * window

    step = 2.0 * math.pi / FFT
    scale = 1.0 / math.sqrt(FFT)
    groups = CHAN // (2 * ROWS)
    phase = (
        lax.broadcasted_iota(jnp.int32, (groups, LANES), 0)
        * lax.broadcasted_iota(jnp.int32, (groups, LANES), 1)
        * (2 * ROWS)
    ) % FFT
    angle = phase.astype(jnp.float32) * step
    ecos_ref[...] = jnp.cos(angle)
    esin_ref[...] = jnp.sin(angle)
    sub = lax.broadcasted_iota(jnp.int32, (ROWS, LANES), 0)
    lane = lax.broadcasted_iota(jnp.int32, (ROWS, LANES), 1)
    half_turns = FFT // LANES // 2
    factors = []
    for h in range(2):
        near = ROWS * (sub % CORES) + sub // CORES + h * ROWS // 2
        angle = ((near * lane) % FFT).astype(jnp.float32) * step
        turns = []
        for j in range(half_turns):
            turn = ((near * (j * LANES)) % FFT).astype(jnp.float32) * step
            turns.append((jnp.cos(turn), jnp.sin(turn)))
        factors.append((jnp.cos(angle) * scale, jnp.sin(angle) * scale, turns))
    odd = lax.broadcasted_iota(jnp.int32, (2 * ROWS, LANES), 0) // CORES % 2 == 1
    sign = jnp.where(odd, -1.0, 1.0).astype(jnp.bfloat16)

    def pair(w, carry):
        ec = ecos_ref[pl.ds(w, 1), :]
        es = esin_ref[pl.ds(w, 1), :]
        bases = [(ec * gcos - es * gsin, es * gcos + ec * gsin) for gcos, gsin, _ in factors]
        row = pl.multiple_of(w * 2 * ROWS, 2 * ROWS)
        for j in range(half_turns):
            real, imag = [], []
            for (bc, bs), (_, _, turns) in zip(bases, factors):
                tc, ts = turns[j]
                real.append(bc * tc - bs * ts if j else bc)
                imag.append(-(bs * tc + bc * ts) if j else -bs)
            for q, value in enumerate((real, imag)):
                value = jnp.concatenate(value, 0).astype(jnp.bfloat16)
                rows = pl.ds(q * CHAN + row, 2 * ROWS)
                tab_ref[rows, j * LANES : (j + 1) * LANES] = value
                tab_ref[rows, (j + half_turns) * LANES : (j + half_turns + 1) * LANES] = value * sign
        return carry

    lax.fori_loop(0, groups, pair, 0)

    for load in loads:
        load.wait()

    pitch = count + ROWS

    def column(j, carry):
        base = pl.multiple_of(j * LANES, LANES)
        cols = pl.ds(base, LANES)
        taps = [jnp.broadcast_to(coef_ref[pl.ds(k, 1), cols], (ROWS, LANES)) for k in range(TAPS)]
        past = []
        for s in range(count):
            past.append(local_ref[:, pl.ds(base + s * FFT, LANES)].astype(jnp.float32))
            total = taps[TAPS - len(past)] * past[0]
            for k in range(1, len(past)):
                total = total + taps[TAPS - len(past) + k] * past[k]
            if s < TAPS - 1:
                head_ref[pl.ds(s * ROWS, ROWS), cols] = total
            else:
                past = past[1:]
            part_ref[pl.ds(s, ROWS, stride=pitch), :] = total
        for a in range(ROWS):
            filt_ref[a * count : (a + 1) * count, cols] = part_ref[a * pitch : a * pitch + count, :].astype(
                jnp.bfloat16
            )
        return carry

    lax.fori_loop(0, FFT // LANES, column, 0)


def prepare(volts):
    inp_local, samples = volts.shape
    count = samples // FFT
    vmem = pl.BlockSpec(memory_space=pltpu.VMEM)
    return pl.pallas_call(
        functools.partial(prepare_kernel, count),
        out_shape=(
            jax.ShapeDtypeStruct((2 * CHAN, FFT), jnp.bfloat16),
            jax.ShapeDtypeStruct((TAPS, FFT), jnp.float32),
            jax.ShapeDtypeStruct((ROWS * count, FFT), jnp.bfloat16),
            jax.ShapeDtypeStruct(((TAPS - 1) * ROWS, FFT), jnp.float32),
        ),
        in_specs=[pl.BlockSpec(memory_space=pltpu.HBM)],
        out_specs=(vmem,) * 4,
        scratch_shapes=[
            pltpu.VMEM((ROWS, samples), jnp.bfloat16),
            pltpu.VMEM(((ROWS + 1) * (count + ROWS), LANES), jnp.float32),
            pltpu.VMEM((CHAN // (2 * ROWS), LANES), jnp.float32),
            pltpu.VMEM((CHAN // (2 * ROWS), LANES), jnp.float32),
            pltpu.SemaphoreType.DMA((LOADS,)),
        ],
        compiler_params=pltpu.CompilerParams(vmem_limit_bytes=VMEM_LIMIT),
        cost_estimate=pl.CostEstimate(flops=8_000_000, bytes_accessed=1_100_000, transcendentals=20_000),
        name="prepare",
    )(pltpu.with_memory_space_constraint(volts, pltpu.HBM))


def spectra_kernel(count, halo_ref, coef_ref, tab_ref, filt_ref, head_ref, out_ref, fixed_ref, row_ref, tile_ref):
    late = TAPS - 1
    first = lax.broadcasted_iota(jnp.int32, (ROWS, LANES), 0) < late
    for j in range(FFT // LANES):
        cols = slice(j * LANES, (j + 1) * LANES)
        before = [
            halo_ref[:, k * FFT + j * LANES : k * FFT + (j + 1) * LANES].astype(jnp.float32) for k in range(late)
        ]
        for s in range(late):
            total = head_ref[s * ROWS : (s + 1) * ROWS, cols]
            for k in range(late - s):
                total = total + coef_ref[k : k + 1, cols] * before[s + k]
            row_ref[pl.ds(s, ROWS, stride=ROWS), :] = total
        for a in range(ROWS):
            own = filt_ref[a * count : a * count + 2 * ROWS, cols].astype(jnp.float32)
            top = jnp.where(first, row_ref[a * ROWS : (a + 1) * ROWS, :], own[:ROWS])
            fixed_ref[a * count : a * count + 2 * ROWS, cols] = jnp.concatenate([top, own[ROWS:]], 0).astype(
                jnp.bfloat16
            )

    chunk = 256
    low = lax.broadcasted_iota(jnp.int32, (chunk, LANES), 1) < LANES // 2
    for h in range(CHAN // chunk):
        parts = [
            lax.dot_general(
                tab_ref[q * CHAN + h * chunk : q * CHAN + (h + 1) * chunk, :],
                fixed_ref[...],
                NT,
                preferred_element_type=jnp.float32,
            )
            for q in range(2)
        ]
        for j in range(ROWS // 2):
            re = parts[0][:, j * LANES : (j + 1) * LANES]
            im = parts[1][:, j * LANES : (j + 1) * LANES]
            tile_ref[pl.ds(2 * j, chunk, stride=ROWS), :] = jnp.where(low, re, pltpu.roll(im, LANES // 2, 1))
            tile_ref[pl.ds(2 * j + 1, chunk, stride=ROWS), :] = jnp.where(
                low, pltpu.roll(re, LANES // 2, 1), im
            )
        out_ref[h * chunk * ROWS : (h + 1) * chunk * ROWS, :] = tile_ref[: chunk * ROWS, :].astype(
            jnp.bfloat16
        )


def make_spectra(halo, coef, table, filtered, head):
    count = filtered.shape[0] // ROWS
    vmem = pl.BlockSpec(memory_space=pltpu.VMEM)
    return pl.pallas_call(
        functools.partial(spectra_kernel, count),
        out_shape=(
            jax.ShapeDtypeStruct((CHAN * ROWS, LANES), jnp.bfloat16),
            jax.ShapeDtypeStruct(filtered.shape, jnp.bfloat16),
        ),
        in_specs=[vmem] * 5,
        out_specs=(vmem, vmem),
        input_output_aliases={3: 1},
        scratch_shapes=[
            pltpu.VMEM(((ROWS + 1) * ROWS, LANES), jnp.float32),
            pltpu.VMEM((257 * ROWS, LANES), jnp.float32),
        ],
        compiler_params=pltpu.CompilerParams(vmem_limit_bytes=VMEM_LIMIT),
        cost_estimate=pl.CostEstimate(flops=1_100_000_000, bytes_accessed=4_000_000, transcendentals=0),
        name="spectra",
    )(halo, coef, table, filtered, head)[0]


def gram_kernel(scale, tiles_ref, out_ref, m_ref, turned_ref, block_ref, sem):
    inputs, depth = m_ref.shape
    block = inputs // 2
    low = lax.broadcasted_iota(jnp.int32, (inputs, LANES), 1) < LANES // 2
    for k in range(depth // LANES):
        cols = slice(k * LANES, (k + 1) * LANES)
        tile = tiles_ref[:, k].reshape(inputs, LANES)
        m_ref[:, cols] = tile
        swapped = pltpu.roll(tile, LANES // 2, 1)
        turned_ref[:, cols] = jnp.where(low, -swapped, swapped)
    copies = []
    for i in range(2):
        rows = pl.ds(i * block, block)
        left = m_ref[rows, :]
        for part, right_ref in enumerate((m_ref, turned_ref)):
            block_ref[part, 0, rows, :] = (
                lax.dot_general(left, right_ref[...], NT, preferred_element_type=jnp.float32) * scale
            )
            copies.append(
                pltpu.make_async_copy(
                    block_ref.at[part, 0, rows], out_ref.at[part, 0, rows], sem.at[2 * i + part]
                )
            )
            copies[-1].start()
    for copy in copies:
        copy.wait()


def make_gram(tiles, time_total):
    chips, slabs, rows, lanes = tiles.shape
    inputs, depth = chips * rows, slabs * lanes
    shape = (2, 1, inputs, inputs)
    return pl.pallas_call(
        functools.partial(gram_kernel, 1.0 / time_total),
        out_shape=jax.ShapeDtypeStruct(shape, jnp.float32),
        in_specs=[pl.BlockSpec(memory_space=pltpu.VMEM)],
        out_specs=pl.BlockSpec(memory_space=pl.ANY),
        scratch_shapes=[
            pltpu.VMEM((inputs, depth), jnp.bfloat16),
            pltpu.VMEM((inputs, depth), jnp.bfloat16),
            pltpu.VMEM(shape, jnp.float32),
            pltpu.SemaphoreType.DMA((4,)),
        ],
        compiler_params=pltpu.CompilerParams(vmem_limit_bytes=VMEM_LIMIT),
        cost_estimate=pl.CostEstimate(flops=1_100_000_000, bytes_accessed=3_200_000, transcendentals=0),
        name="gram",
    )(tiles)


def on_device(volts):
    inp_local, samples = volts.shape
    count = samples // FFT
    slabs = lax.axis_size("tm")
    chips = lax.axis_size("chip")
    halo = lax.ppermute(
        volts[:, samples - (TAPS - 1) * FFT :], "tm", [(i, i + 1) for i in range(slabs - 1)]
    )
    table, coef, filtered, head = prepare(volts)
    tiles = make_spectra(halo, coef, table, filtered, head)
    tiles = tiles.reshape(CHAN, inp_local, 2 * count)
    tiles = lax.all_to_all(tiles, ("chip", "tm", "core"), split_axis=0, concat_axis=0, tiled=True)
    return make_gram(tiles.reshape(chips, slabs, CORES * inp_local, 2 * count), slabs * count)


def solution(mesh):
    groups, slabs = mesh.devices.shape
    split = Mesh(mesh.devices.reshape(groups // CORES, CORES, slabs), ("chip", "core", "tm"))
    return jax.shard_map(
        on_device,
        mesh=split,
        in_specs=(P(("chip", "core"), "tm"),),
        out_specs=P(None, ("chip", "core", "tm"), None, None),
        check_vma=False,
    )
```
